256 devices in a mesh: rowa: 8 (over z), rowb: 4 (over y), tm: 8 (over x, core).
Axes of the slice: x: 4, y: 4, z: 8, core: 2. Of those that a mesh axis runs over, the one named last changes fastest.
Arguments:
- snapshots: bfloat16 [2048, 131072], P('tm', ('rowa', 'rowb')), may hold values from -4 to 4
- basis: bfloat16 [40, 131072], P(None, ('rowa', 'rowb')), may hold values from -0.015625 to 0.015625
Outputs:
- operators: float32 [40, 861], replicated
- residual: float32 [40, 2048], P(None, 'tm')
The draws below stay inside these ranges and needn't reach their ends.
All inputs are finite; a program needn't handle non-finite values.
Results may differ from the reference program's by a relative error of at most 0.0017.
Values sent between devices are 32-bit elements; how exact they have to be, the bound alone decides.
A program may use at most 128 MiB of HBM per device.

```python
import math
import jax
import jax.numpy as jnp
import numpy as np
from jax import lax

R = 40
ROWS = 131072
SNAPS = 2048


def draw_snapshots(key, part):
    key = jax.random.fold_in(key, 7)
    key_freq, key_phase, key_noise = jax.random.split(key, 3)
    pairs = R * 2 // 5
    times = jnp.arange(SNAPS, dtype=jnp.float32)[:, None]
    omega = jax.random.uniform(key_freq, (pairs,), jnp.float32, 0.03, 0.35)
    phase = jax.random.uniform(key_phase, (pairs,), jnp.float32, -math.pi, math.pi)
    angles = times * omega[None, :] + phase[None, :]
    cosines = jnp.cos(angles)
    sines = jnp.sin(angles)
    linear_part = jnp.stack([cosines, sines], axis=2).reshape(SNAPS, 2 * pairs)
    first_osc = jnp.arange(R - 2 * pairs) % pairs
    second_osc = (first_osc + 1) % pairs
    product_part = 2.0 * cosines[:, first_osc] * cosines[:, second_osc]
    latent = jnp.concatenate([1.4 * linear_part, product_part], axis=1)
    column_mode = jnp.arange(ROWS) % R
    signal = latent[:, column_mode]
    noise = 0.5 * jnp.clip(jax.random.normal(key_noise, (SNAPS, ROWS), jnp.float32), -4.0, 4.0)
    values = signal + noise
    return values.astype(jnp.bfloat16)


def levels(stream_key, extent, cuts, low, top_value):
    def one(position, parts):
        steps = jax.random.uniform(jax.random.fold_in(jax.random.fold_in(stream_key, 6), position), (parts,), jnp.float32, low / len(cuts), top_value / len(cuts))
        return jnp.repeat(jnp.exp(steps), extent[position] // parts).reshape((-1,) + (1,) * (len(extent) - position - 1))

    level = one(*cuts[0])
    for cut in cuts[1:]:
        level = level * one(*cut)
    return level


def gaussian(own_key, dims, spread, reach, cuts=(), kind=jnp.bfloat16):
    entries = spread * jax.random.normal(own_key, dims, jnp.float32)
    if cuts:
        entries = entries * levels(own_key, dims, cuts, -0.22, 0.18)
    return jnp.clip(entries, -reach, reach).astype(kind)


def setup_inputs(seed: int = 0) -> dict:
    seeds = jax.random.split(jax.random.key(seed), 3)
    snapshots = draw_snapshots(jax.random.fold_in(seeds[2], 71), 0)
    basis = gaussian(seeds[1], (R, ROWS), ROWS ** -0.5, 0.015625, ((1, 32),))
    return {"snapshots": snapshots, "basis": basis}


def features(current):
    modes = current.shape[1]
    first_index, second_index = np.triu_indices(modes)
    quadratic = current[:, first_index] * current[:, second_index]
    ones_column = jnp.ones((current.shape[0], 1), jnp.float32)
    return jnp.concatenate([current, quadratic, ones_column], axis=1)

def penalty_diag(modes, columns, snaps):
    index = jnp.arange(columns)
    middle = (index >= modes) & (index < columns - 1)
    return jnp.where(middle, 0.1 * snaps, 0.01 * snaps).astype(jnp.float32)

def solve_operators(gram, rhs, modes, snaps):
    columns = gram.shape[0]
    system = gram + jnp.diag(penalty_diag(modes, columns, snaps))
    factor = jnp.linalg.cholesky(system)
    return jax.scipy.linalg.cho_solve((factor, True), rhs)

def reference(snapshots, basis):
    projected = lax.dot_general(snapshots.astype(jnp.float32), basis.astype(jnp.float32), (((1,), (1,)), ((), ())), preferred_element_type=jnp.float32)
    following = jnp.concatenate([projected[1:], jnp.zeros((1, R), jnp.float32)], axis=0)
    design = features(projected)
    keep = (jnp.arange(SNAPS) < SNAPS - 1).astype(jnp.float32)[:, None]
    weighted = design * keep
    gram = lax.dot_general(weighted.astype(jnp.float32), design.astype(jnp.float32), (((0,), (0,)), ((), ())), precision=lax.Precision.HIGHEST, preferred_element_type=jnp.float32)
    rhs = lax.dot_general(weighted.astype(jnp.float32), following.astype(jnp.float32), (((0,), (0,)), ((), ())), precision=lax.Precision.HIGHEST, preferred_element_type=jnp.float32)
    coefficients = solve_operators(gram, rhs, R, SNAPS)
    fitted = jnp.dot(design.astype(jnp.float32), coefficients.astype(jnp.float32), precision=lax.Precision.HIGHEST, preferred_element_type=jnp.float32)
    residual = ((following - fitted) * keep).T
    return (coefficients.T, residual)
```

```python
import functools
import numpy as np
import jax, jax.numpy as jnp
from jax import lax
from jax.experimental import pallas as pl
from jax.experimental.pallas import tpu as pltpu
from jax.sharding import PartitionSpec as P

MODES=40; COLS=861; PAD=896; BLK=128; NB=7; SNAPS=2048; RHS=896
HALF=MODES//2
NN=(((1,),(0,)),((),())); NT=(((1,),(1,)),((),())); TN=(((0,),(0,)),((),()))

def row_of_column():
    rows=np.full((1,PAD),-1,np.int32)
    rows[0,:MODES]=HALF*MODES+np.arange(MODES)
    at=MODES
    for i in range(MODES):
        for j in range(i,MODES):
            d=j-i
            if d<HALF: r=d*MODES+i
            elif d==HALF: r=(HALF+1)*MODES+i
            else: r=(MODES-d)*MODES+j
            rows[0,at]=r; at+=1
    rows[0,at]=COLS-1
    return rows

def split(x):
    hi=x.astype(jnp.bfloat16)
    return hi,(x-hi.astype(jnp.float32)).astype(jnp.bfloat16)

def dot(a,b,dims):
    return lax.dot_general(a,b,dims,preferred_element_type=jnp.float32)

def dot3(a,b,dims):
    ah,al=a; bh,bl=b
    return dot(ah,bh,dims)+(dot(ah,bl,dims)+dot(al,bh,dims))

def spread_row(x,k): return jnp.broadcast_to(x[k:k+1,:],(8,BLK))
def spread_col(x,c): return jnp.broadcast_to(x[:,c:c+1],(8,BLK))

def inverse(a):
    a=list(a)
    sub=lax.broadcasted_iota(jnp.int32,(8,BLK),0)
    lane=lax.broadcasted_iota(jnp.int32,(8,BLK),1)
    for s in range(16):
        R=a[s]
        C=[spread_col(R,8*s+k) for k in range(8)]
        inblk=(lane>=8*s)&(lane<8*s+8)
        R=jnp.where(inblk,jnp.where(lane-8*s==sub,1.0,0.0),R)
        for k in range(8):
            on=sub==k
            r=1.0/spread_row(C[k],k)
            Ck=jnp.where(on,-1.0,C[k])
            for j in range(k+1,8):
                C[j]=jnp.where(on,0.0,C[j])-Ck*(spread_row(C[j],k)*r)
            R=jnp.where(on,0.0,R)-Ck*(spread_row(R,k)*r)
        V=[spread_row(R,k) for k in range(8)]
        for i in range(16):
            if i==s: continue
            x=a[i]
            acc=jnp.where(inblk,0.0,x)
            for k in range(8):
                acc=acc-spread_col(x,8*s+k)*V[k]
            a[i]=acc
        a[s]=R
    return jnp.concatenate(a,axis=0)

def fit_kernel(here_fn,upto,p_ref,rowof_ref,op_ref,res_ref,twice,hi,lo,sys,sol):
    f32=jnp.float32
    lane=lax.broadcasted_iota(jnp.int32,(1,SNAPS),1)
    keep=(lane<SNAPS-1)
    proj=p_ref[...]
    F=jnp.where(keep,jnp.concatenate([proj[:,1:],proj[:,:1]],axis=1),0.0)
    Pm=jnp.where(keep,proj,0.0)
    twice[0:MODES,:]=Pm
    twice[MODES:2*MODES,:]=Pm
    def put(at,x):
        h,l=split(x)
        hi[at:at+x.shape[0],:]=h
        lo[at:at+x.shape[0],:]=l
    for d in range(0,HALF,2):
        put(d*MODES,jnp.concatenate([twice[0:MODES,:]*twice[d:d+MODES,:],twice[0:MODES,:]*twice[d+1:d+1+MODES,:]],axis=0))
    sub24=lax.broadcasted_iota(jnp.int32,(24,SNAPS),0)
    last=jnp.where(sub24<HALF,twice[0:24,:]*twice[HALF:HALF+24,:],jnp.where((sub24==HALF)&(lax.broadcasted_iota(jnp.int32,(24,SNAPS),1)<SNAPS-1),1.0,0.0))
    put(800,jnp.concatenate([Pm,last,jnp.zeros((32,SNAPS),f32),F,jnp.zeros((88,SNAPS),f32)],axis=0))
    if upto==1: return
    for I in range(4):
        for J in range(I,4):
            r,c=slice(256*I,256*I+256),slice(256*J,256*J+256)
            sys[r,c]=dot3((hi[r,:],lo[r,:]),(hi[c,:],lo[c,:]),NT)
    if upto==2: return
    sub=lax.broadcasted_iota(jnp.int32,(BLK,BLK),0)
    diag=sub==lax.broadcasted_iota(jnp.int32,(BLK,BLK),1)
    for k in range(NB):
        at=slice(BLK*k,BLK*k+BLK)
        row=sub+BLK*k
        pen=jnp.where((row<800)|((row>=840)&(row<860)),0.1*SNAPS,jnp.where(row<COLS,0.01*SNAPS,1.0)).astype(f32)
        D=sys[at,at]+jnp.where(diag,pen,0.0)
        inv=inverse([D[8*i:8*i+8,:] for i in range(16)])
        rest=slice(BLK*k+BLK,PAD+BLK)
        R=sys[at,rest]
        Rs=split(R)
        W=dot3(split(inv),Rs,NN)
        Ws=split(W)
        sys[at,rest]=W
        for i in range(k+1,NB):
            o=BLK*(i-k-1)
            sys[BLK*i:BLK*i+BLK,BLK*i:]=sys[BLK*i:BLK*i+BLK,BLK*i:]-dot3((Rs[0][:,o:o+BLK],Rs[1][:,o:o+BLK]),(Ws[0][:,o:],Ws[1][:,o:]),TN)
    if upto==3: return
    for k in range(NB-1,-1,-1):
        at=slice(BLK*k,BLK*k+BLK)
        x=sys[at,RHS:]
        if k<NB-1:
            x=x-dot3(split(sys[at,BLK*k+BLK:RHS]),split(sol[BLK*k+BLK:,:]),NN)
        sol[at,:]=x
    if upto==4: return
    X=sol[...]
    Xh,Xl=split(X)
    here=pl.ds(here_fn(),256)
    fit=dot3((Xh,Xl),(hi[0:PAD,here],lo[0:PAD,here]),TN)
    ahead=hi[RHS:RHS+48,here].astype(f32)+lo[RHS:RHS+48,here].astype(f32)
    res_ref[...]=(ahead-fit[0:48,:])[0:MODES,:]
    X3=(X-Xh.astype(f32)-Xl.astype(f32)).astype(jnp.bfloat16)
    perm=jnp.where(lax.broadcasted_iota(jnp.int32,(PAD,PAD),0)==rowof_ref[...],1.0,0.0).astype(jnp.bfloat16)
    out=dot(Xh,perm,TN)+(dot(Xl,perm,TN)+dot(X3,perm,TN))
    op_ref[...]=out[0:MODES,0:COLS]

def fit(p,here_fn,upto=9):

    return pl.pallas_call(
        functools.partial(fit_kernel,here_fn,upto),
        out_shape=(jax.ShapeDtypeStruct((MODES,COLS),jnp.float32),jax.ShapeDtypeStruct((MODES,256),jnp.float32)),
        scratch_shapes=[pltpu.VMEM((2*MODES,SNAPS),jnp.float32),pltpu.VMEM((1024,SNAPS),jnp.bfloat16),pltpu.VMEM((1024,SNAPS),jnp.bfloat16),
          pltpu.VMEM((1024,1024),jnp.float32),pltpu.VMEM((PAD,BLK),jnp.float32)],
        compiler_params=pltpu.CompilerParams(vmem_limit_bytes=56*2**20),
        name="fit",
    )(p,jnp.asarray(row_of_column()))
MESH=pl.DeviceIdType.MESH
TILES=10
PLANE=32
CHUNK=1024

def gather_kernel(snap_ref,basis_ref,p_ref,snap,basis,part,terms,block,load_sem,scatter_send,scatter_recv,spread_send,spread_recv,time_send,time_recv):
    tm=lax.axis_index("tm")
    rowa=lax.axis_index("rowa")
    rowb=lax.axis_index("rowb")
    here=rowa*4+rowb
    core=lax.rem(tm,2)
    chunks=snap.shape[1]//CHUNK
    loads=[]
    for c in range(chunks):
        at=pl.ds(c*CHUNK,CHUNK)
        a=pltpu.make_async_copy(snap_ref.at[:,at],snap.at[:,at],load_sem.at[0,c])
        b=pltpu.make_async_copy(basis_ref.at[:,at],basis.at[:,at],load_sem.at[1,c])
        a.start(); b.start()
        loads.append((a,b))
    barrier=pltpu.get_barrier_semaphore()
    def plane_id(i):
        q=lax.rem(here+i,PLANE)
        return {"rowa":q//4,"rowb":lax.rem(q,4)}
    def time_id(i):
        return {"tm":lax.rem(tm+i,8)}
    def greet(i,_):
        pl.semaphore_signal(barrier,inc=1,device_id=plane_id(i),device_id_type=MESH)
        return 0
    lax.fori_loop(1,PLANE,greet,0)
    for i in range(1,8):
        pl.semaphore_signal(barrier,inc=1,device_id=time_id(i),device_id_type=MESH)
    total=jnp.zeros((MODES,256),jnp.float32)
    for c in range(chunks):
        for x in loads[c]: x.wait()
        total=total+lax.dot_general(basis[:,c*CHUNK:(c+1)*CHUNK],snap[:,c*CHUNK:(c+1)*CHUNK],NT,preferred_element_type=jnp.float32)
    for t in range(TILES):
        g,h=t//2,t%2
        part[t]=total[8*g:8*g+8,128*h:128*h+128]
    pl.semaphore_wait(barrier,PLANE-1+7)
    def owner(t): return 3*t+core
    def scatter(t):
        q=owner(t)
        return pltpu.make_async_remote_copy(src_ref=part.at[t],dst_ref=terms.at[here],send_sem=scatter_send.at[t],recv_sem=scatter_recv,device_id={"rowa":q//4,"rowb":lax.rem(q,4)},device_id_type=MESH)
    def lanes(h): return pl.ds(pl.multiple_of(256*tm+128*h,128),128)
    def spread(t,i):
        g,h=t//2,t%2
        ref=block.at[8*g:8*g+8,lanes(h)]
        return pltpu.make_async_remote_copy(src_ref=ref,dst_ref=ref,send_sem=spread_send,recv_sem=spread_recv.at[t],device_id=plane_id(i),device_id_type=MESH)
    for t in range(TILES):
        @pl.when(owner(t)!=here)
        def _(): scatter(t).start()
    for t in range(TILES):
        @pl.when(owner(t)==here)
        def _():
            g,h=t//2,t%2
            pltpu.make_async_copy(terms.at[0:PLANE-1],terms.at[0:PLANE-1],scatter_recv).wait()
            terms[here]=part[t]
            sums=terms[0]
            for q in range(1,PLANE): sums=sums+terms[q]
            block[8*g:8*g+8,lanes(h)]=sums
            def send(i,_):
                spread(t,i).start()
                return 0
            lax.fori_loop(1,PLANE,send,0)
    for t in range(TILES):
        @pl.when(owner(t)!=here)
        def _(): spread(t,1).wait_recv()
    mine=block.at[:,pl.ds(pl.multiple_of(256*tm,256),256)]
    copies=[]
    for i in range(1,8):
        c=pltpu.make_async_remote_copy(src_ref=mine,dst_ref=mine,send_sem=time_send.at[i-1],recv_sem=time_recv.at[i-1],device_id=time_id(i),device_id_type=MESH)
        c.start()
        copies.append(c)
    for t in range(TILES):
        @pl.when(owner(t)!=here)
        def _(): scatter(t).wait_send()
        @pl.when(owner(t)==here)
        def _(): pltpu.make_async_copy(terms.at[0:PLANE-1],terms.at[0:PLANE-1],spread_send).wait()
    for i in range(1,8):
        src=lax.rem(tm+8-i,8)
        theirs=block.at[:,pl.ds(pl.multiple_of(256*src,256),256)]
        pltpu.make_async_remote_copy(src_ref=theirs,dst_ref=theirs,send_sem=time_send.at[i-1],recv_sem=time_recv.at[i-1],device_id=time_id(i),device_id_type=MESH).wait_recv()
        copies[i-1].wait_send()
    p_ref[...]=block[...]

def gather(snapshots,basis):
    return pl.pallas_call(
        gather_kernel,
        out_shape=jax.ShapeDtypeStruct((MODES,SNAPS),jnp.float32),
        in_specs=[pl.BlockSpec(memory_space=pl.ANY)]*2,
        out_specs=pl.BlockSpec(memory_space=pltpu.VMEM),
        scratch_shapes=[
            pltpu.VMEM(snapshots.shape,jnp.bfloat16),
            pltpu.VMEM(basis.shape,jnp.bfloat16),
            pltpu.VMEM((TILES,8,128),jnp.float32),
            pltpu.VMEM((PLANE,8,128),jnp.float32),
            pltpu.VMEM((MODES,SNAPS),jnp.float32),
            pltpu.SemaphoreType.DMA((2,snapshots.shape[1]//CHUNK)),
            pltpu.SemaphoreType.DMA((TILES,)),
            pltpu.SemaphoreType.DMA,
            pltpu.SemaphoreType.DMA,
            pltpu.SemaphoreType.DMA((TILES,)),
            pltpu.SemaphoreType.DMA((7,)),
            pltpu.SemaphoreType.DMA((7,)),
        ],
        compiler_params=pltpu.CompilerParams(collective_id=0,has_side_effects=True,vmem_limit_bytes=32*2**20),
        name="gather",
    )(snapshots,basis)

def on_device(snapshots,basis):
    p=gather(snapshots,basis)
    return fit(p,lambda: pl.multiple_of(lax.axis_index("tm")*256,256))

def solution(mesh):
    return jax.shard_map(on_device,mesh=mesh,in_specs=(P("tm",("rowa","rowb")),P(None,("rowa","rowb"))),out_specs=(P(),P(None,"tm")),check_vma=False)
```

```python
import functools

import numpy as np
import jax, jax.numpy as jnp
from jax import lax
from jax.experimental import pallas as pl
from jax.experimental.pallas import tpu as pltpu
from jax.sharding import PartitionSpec as P

MODES=40; COLS=861; PAD=896; BLK=128; NB=7; SNAPS=2048; RHS=896
HALF=MODES//2
NN=(((1,),(0,)),((),())); NT=(((1,),(1,)),((),())); TN=(((0,),(0,)),((),()))

def row_of_column():
    rows=np.full((1,PAD),-1,np.int32)
    rows[0,:MODES]=HALF*MODES+np.arange(MODES)
    at=MODES
    for i in range(MODES):
        for j in range(i,MODES):
            d=j-i
            if d<HALF: r=d*MODES+i
            elif d==HALF: r=(HALF+1)*MODES+i
            else: r=(MODES-d)*MODES+j
            rows[0,at]=r; at+=1
    rows[0,at]=COLS-1
    return rows

def split(x):
    hi=x.astype(jnp.bfloat16)
    return hi,(x-hi.astype(jnp.float32)).astype(jnp.bfloat16)

def dot(a,b,dims):
    return lax.dot_general(a,b,dims,preferred_element_type=jnp.float32)

def dot3(a,b,dims):
    ah,al=a; bh,bl=b
    return dot(ah,bh,dims)+(dot(ah,bl,dims)+dot(al,bh,dims))

def spread_row(x,k): return jnp.broadcast_to(x[k:k+1,:],(8,BLK))
def spread_col(x,c): return jnp.broadcast_to(x[:,c:c+1],(8,BLK))

def row_of(x,k): return spread_row(x[k//8],k%8)

def eliminate(cols,rows):
    n=len(cols)
    sub=lax.broadcasted_iota(jnp.int32,(8,BLK),0)
    scale=[jnp.zeros((8,BLK),jnp.float32) for _ in rows]
    def step(k,r,rows):
        on=sub==k%8
        m=list(cols[k])
        m[k//8]=jnp.where(on,0.0,m[k//8])
        m=[x*r for x in m]
        scale[k//8]=jnp.where(on,r,scale[k//8])
        def less(x):
            t=row_of(x,k)
            return [x[q]-m[q]*t for q in range(len(x))]
        for j in range(k+1,n): cols[j]=less(cols[j])
        return less(rows)
    for k in range(0,n,2):
        p=row_of(cols[k],k)
        det=p*row_of(cols[k+1],k+1)-row_of(cols[k],k+1)*row_of(cols[k+1],k)
        r,r2=1.0/p,p*(1.0/det)
        rows=step(k,r,rows)
        rows=step(k+1,r2,rows)
    return [rows[q]*scale[q] for q in range(len(rows))]

def inverse(a):
    a=list(a)
    bf=jnp.bfloat16
    sub=lax.broadcasted_iota(jnp.int32,(8,BLK),0)
    lane=lax.broadcasted_iota(jnp.int32,(8,BLK),1)
    for s in range(8):
        at,nxt=(2*s,2*s+1),((2*s+2,2*s+3) if s<7 else ())
        inblk=(lane>=16*s)&(lane<16*s+16)
        cols=[[spread_col(a[i],16*s+k) for i in at] for k in range(16)]
        rows=[jnp.where(inblk,jnp.where(lane-16*s==sub+8*q,1.0,0.0),a[i]) for q,i in enumerate(at)]
        rows=eliminate(cols,rows)
        def pad(v):
            return jnp.concatenate(([jnp.zeros((16*s,BLK),bf)] if s else [])+[v]+([jnp.zeros((112-16*s,BLK),bf)] if s<7 else []),axis=0)
        far=[i for i in range(16) if i not in at+nxt]
        upd=dot3(split(jnp.concatenate([a[i] for i in far],axis=0)),tuple(pad(v) for v in split(jnp.concatenate(rows,axis=0))),NN)
        new=list(a)
        for n,i in enumerate(far):
            new[i]=jnp.where(inblk,0.0,a[i])-upd[8*n:8*n+8]
        if nxt:
            V=[row_of(rows,k) for k in range(16)]
        for i in nxt:
            p=[spread_col(a[i],16*s+k)*V[k] for k in range(16)]
            while len(p)>1: p=[p[2*q]+p[2*q+1] for q in range(len(p)//2)]
            new[i]=jnp.where(inblk,0.0,a[i])-p[0]
        for q,i in enumerate(at): new[i]=rows[q]
        a=new
    return jnp.concatenate(a,axis=0)


MESH=pl.DeviceIdType.MESH
TILES=10
PLANE=32
ORDER=(0,1,2,3,7,6,5,4)
AT=(5,6,7)
CHUNK=1024
WIDE=256
PIECES=[(i,j) for i in range(4) for j in range(i,3)]+[(i,3) for i in range(4)]

def put(hi,lo,at,cols,x):
    h,l=split(x)
    hi[at:at+x.shape[0],cols]=h
    lo[at:at+x.shape[0],cols]=l

def kept(first):
    return first+lax.broadcasted_iota(jnp.int32,(1,WIDE),1)<SNAPS-1

def features(hi,lo,twice,slot,block,first):
    keep=kept(first)
    now=jnp.where(keep,block,0.0)
    twice[0:MODES,:]=now
    twice[MODES:2*MODES,:]=now
    cols=pl.ds(pl.multiple_of(WIDE*slot,WIDE),WIDE)
    for d in range(0,HALF,2):
        put(hi,lo,d*MODES,cols,jnp.concatenate([now*twice[d:d+MODES,:],now*twice[d+1:d+1+MODES,:]],axis=0))
    sub=lax.broadcasted_iota(jnp.int32,(24,WIDE),0)
    last=jnp.where(sub<HALF,twice[0:24,:]*twice[HALF:HALF+24,:],jnp.where((sub==HALF)&keep,1.0,0.0))
    put(hi,lo,800,cols,jnp.concatenate([now,last,jnp.zeros((32,WIDE),jnp.float32)],axis=0))

def targets(hi,lo,slot,block,edge,first):
    lane=lax.broadcasted_iota(jnp.int32,(MODES,WIDE),1)
    ahead=jnp.concatenate([block[:,1:],block[:,:1]],axis=1)
    ahead=jnp.where(lane==WIDE-1,jnp.broadcast_to(edge[:,0:1],(MODES,WIDE)),ahead)
    ahead=jnp.where(kept(first),ahead,0.0)
    cols=slice(WIDE*slot,WIDE*slot+WIDE)
    put(hi,lo,RHS,cols,jnp.concatenate([ahead,jnp.zeros((88,WIDE),jnp.float32)],axis=0))

def product(hi,lo,piece):
    r,c=(slice(WIDE*x,WIDE*x+WIDE) for x in piece)
    return dot3((hi[r,:],lo[r,:]),(hi[c,:],lo[c,:]),NT)

def solve(sys,sol,before):
    sub=lax.broadcasted_iota(jnp.int32,(BLK,BLK),0)
    diag=sub==lax.broadcasted_iota(jnp.int32,(BLK,BLK),1)
    for k in range(NB):
        at=slice(BLK*k,BLK*k+BLK)
        row=sub+BLK*k
        pen=jnp.where((row<800)|((row>=840)&(row<860)),0.1*SNAPS,jnp.where(row<COLS,0.01*SNAPS,1.0)).astype(jnp.float32)
        D=sys[at,at]+jnp.where(diag,pen,0.0)
        inv=inverse([D[8*i:8*i+8,:] for i in range(16)])
        before(k)
        rest=slice(BLK*k+BLK,PAD+BLK)
        Rs=split(sys[at,rest])
        W=dot3(split(inv),Rs,NN)
        Ws=split(W)
        sys[at,rest]=W
        for i in range(k+1,NB):
            o=BLK*(i-k-1)
            sys[BLK*i:BLK*i+BLK,BLK*i:]=sys[BLK*i:BLK*i+BLK,BLK*i:]-dot3((Rs[0][:,o:o+BLK],Rs[1][:,o:o+BLK]),(Ws[0][:,o:],Ws[1][:,o:]),TN)
    for k in range(NB-1,-1,-1):
        at=slice(BLK*k,BLK*k+BLK)
        x=sys[at,RHS:]
        if k<NB-1:
            x=x-dot3(split(sys[at,BLK*k+BLK:RHS]),split(sol[BLK*k+BLK:,:]),NN)
        sol[at,:]=x

def kernel(snap_ref,basis_ref,rowof_ref,op_ref,res_ref,
           snap,basis,part,terms,blocks,edges,twice,hi,lo,mine,peer,sys,sol,perm,
           load_sem,scatter_send,scatter_recv,spread_send,spread_recv,time_send,time_recv,edge_send,edge_recv,sum_send,sum_recv):
    tm=lax.axis_index("tm")
    rowa=lax.axis_index("rowa")
    rowb=lax.axis_index("rowb")
    here=rowa*4+rowb
    x,core=tm//2,lax.rem(tm,2)
    chunks=snap.shape[1]//CHUNK
    loads=[]
    for c in range(chunks):
        at=pl.ds(c*CHUNK,CHUNK)
        pair=(pltpu.make_async_copy(snap_ref.at[:,at],snap.at[:,at],load_sem.at[0,c]),
              pltpu.make_async_copy(basis_ref.at[:,at],basis.at[:,at],load_sem.at[1,c]))
        for y in pair: y.start()
        loads.append(pair)
    def plane_id(q): return {"rowa":q//4,"rowb":lax.rem(q,4)}
    def time_id(i): return {"tm":lax.rem(tm+i,8)}
    def owner(t):
        return 4*(AT[t//4]+core*(11-2*AT[t//4]))+t%4
    turn=lax.rem(rowa+core*(11-2*rowa)+3,8)
    tile=4*turn+rowb
    owns=tile<TILES
    barrier=pltpu.get_barrier_semaphore()
    def greet(device):
        pl.semaphore_signal(barrier,inc=1,device_id=device,device_id_type=MESH)
    @pl.when(owns)
    def _():
        for a in (4,5,6,7,3,2,1,0):
            for b in range(4):
                @pl.when(4*a+b!=here)
                def _(): greet({"rowa":a,"rowb":b})
    @pl.when(jnp.logical_not(owns))
    def _():
        for t in range(TILES): greet(plane_id(owner(t)))
    for i in range(1,8): greet(time_id(i))
    total=jnp.zeros((MODES,WIDE),jnp.float32)
    for c in range(chunks):
        for y in loads[c]: y.wait()
        at=slice(c*CHUNK,c*CHUNK+CHUNK)
        total=total+dot(basis[:,at],snap[:,at],NT)
    for t in range(TILES):
        g,h=t//2,t%2
        part[t]=total[8*g:8*g+8,128*h:128*h+128]
    @pl.when(owns)
    def _(): pl.semaphore_wait(barrier,PLANE-1+7)
    @pl.when(jnp.logical_not(owns))
    def _(): pl.semaphore_wait(barrier,TILES+7)

    def scatter(t):
        return pltpu.make_async_remote_copy(src_ref=part.at[t],dst_ref=terms.at[here],send_sem=scatter_send.at[t],recv_sem=scatter_recv,device_id=plane_id(owner(t)),device_id_type=MESH)
    def spread(a,b):
        ref=blocks.at[x,pl.ds(pl.multiple_of(8*(tile//2),8),8),pl.ds(pl.multiple_of(128*lax.rem(tile,2),128),128)]
        return pltpu.make_async_remote_copy(src_ref=ref,dst_ref=ref,send_sem=spread_send,recv_sem=spread_recv.at[tile],device_id={"rowa":a,"rowb":b},device_id_type=MESH)
    for t in range(TILES):
        @pl.when(owner(t)!=here)
        def _(): scatter(t).start()
    @pl.when(owns)
    def _():
        pltpu.make_async_copy(terms.at[0:PLANE-1],terms.at[0:PLANE-1],scatter_recv).wait()
        terms[here]=part[tile]
        sums=[terms[q] for q in range(PLANE)]
        while len(sums)>1: sums=[sums[2*q]+sums[2*q+1] for q in range(len(sums)//2)]
        blocks[x,pl.ds(pl.multiple_of(8*(tile//2),8),8),pl.ds(pl.multiple_of(128*lax.rem(tile,2),128),128)]=sums[0]
        for a in ORDER:
            for b in range(4):
                @pl.when(4*a+b!=here)
                def _(): spread(a,b).start()
    perm[...]=jnp.where(lax.broadcasted_iota(jnp.int32,(PAD,PAD),0)==rowof_ref[...],1.0,0.0).astype(jnp.bfloat16)
    for t in range(TILES):
        @pl.when(owner(t)!=here)
        def _():
            ref=blocks.at[x,8*(t//2):8*(t//2)+8,128*(t%2):128*(t%2)+128]
            pltpu.make_async_remote_copy(src_ref=ref,dst_ref=ref,send_sem=spread_send,recv_sem=spread_recv.at[t],device_id=plane_id(owner(t)),device_id_type=MESH).wait_recv()

    def to_same(d):
        ref=blocks.at[x]
        return pltpu.make_async_remote_copy(src_ref=ref,dst_ref=ref,send_sem=time_send.at[d-1],recv_sem=time_recv.at[d-1],device_id={"tm":2*lax.rem(x+d,4)+core},device_id_type=MESH)
    for d in (2,1,3): to_same(d).start()
    def to_other():
        return pltpu.make_async_remote_copy(src_ref=blocks.at[:,:,0:128],dst_ref=edges,send_sem=edge_send,recv_sem=edge_recv,device_id={"tm":tm+1-2*core},device_id_type=MESH)
    def arrival(d):
        ref=blocks.at[lax.rem(x+4-d,4)]
        return pltpu.make_async_remote_copy(src_ref=ref,dst_ref=ref,send_sem=time_send.at[d-1],recv_sem=time_recv.at[d-1],device_id={"tm":2*lax.rem(x+d,4)+core},device_id_type=MESH)
    def own(of): features(hi,lo,twice,of,blocks[of],WIDE*(2*of+core))
    own(x)
    for d in (1,2,3): arrival(d).wait_recv()
    to_other().start()
    for of in range(4):
        @pl.when(of!=x)
        def _(): own(of)
    def swap(n):
        return pltpu.make_async_remote_copy(src_ref=mine.at[n],dst_ref=peer.at[n],send_sem=sum_send.at[n],recv_sem=sum_recv.at[n],device_id={"tm":tm+1-2*core},device_id_type=MESH)
    for n,piece in enumerate(PIECES):
        if piece==(0,3):
            to_other().wait_recv()
            for of in range(4): targets(hi,lo,of,blocks[of],edges[lax.rem(of+core,4)],WIDE*(2*of+core))
        mine[n]=product(hi,lo,piece)
        swap(n).start()
    def merge(n):
        i,j=PIECES[n]
        swap(n).wait_recv()
        sys[WIDE*i:WIDE*i+WIDE,WIDE*j:WIDE*j+WIDE]=mine[n]+peer[n]
    merge(0)
    def before(k):
        if k==0:
            for n in range(1,len(PIECES)): merge(n)
    solve(sys,sol,before)

    X=sol[...]
    Xs=split(X)
    cols=pl.ds(pl.multiple_of(WIDE*x,WIDE),WIDE)
    fit=dot3(Xs,(hi[0:PAD,cols],lo[0:PAD,cols]),TN)
    ahead=hi[RHS:RHS+48,cols].astype(jnp.float32)+lo[RHS:RHS+48,cols].astype(jnp.float32)
    res_ref[...]=(ahead-fit[0:48,:])[0:MODES,:]
    out=dot(Xs[0],perm[...],TN)+dot(Xs[1],perm[...],TN)
    op_ref[...]=out[0:MODES,0:COLS]
    for t in range(TILES):
        @pl.when(owner(t)!=here)
        def _(): scatter(t).wait_send()
    @pl.when(owns)
    def _(): pltpu.make_async_copy(terms.at[0:PLANE-1],terms.at[0:PLANE-1],spread_send).wait()
    for d in (1,2,3): to_same(d).wait_send()
    to_other().wait_send()
    for n in range(len(PIECES)): swap(n).wait_send()

def on_device(snapshots,basis):
    f32,bf=jnp.float32,jnp.bfloat16
    dma=pltpu.SemaphoreType.DMA
    n=len(PIECES)
    outs=pl.pallas_call(
        kernel,
        out_shape=(jax.ShapeDtypeStruct((MODES,COLS),f32),jax.ShapeDtypeStruct((MODES,WIDE),f32)),
        in_specs=[pl.BlockSpec(memory_space=pltpu.HBM)]*2+[pl.BlockSpec(memory_space=pltpu.VMEM)],
        out_specs=(pl.BlockSpec(memory_space=pltpu.VMEM),)*2,
        scratch_shapes=[
            pltpu.VMEM(snapshots.shape,bf),pltpu.VMEM(basis.shape,bf),
            pltpu.VMEM((TILES,8,128),f32),pltpu.VMEM((PLANE,8,128),f32),
            pltpu.VMEM((4,MODES,WIDE),f32),pltpu.VMEM((4,MODES,128),f32),
            pltpu.VMEM((2*MODES,WIDE),f32),
            pltpu.VMEM((1024,4*WIDE),bf),pltpu.VMEM((1024,4*WIDE),bf),
            pltpu.VMEM((n,WIDE,WIDE),f32),pltpu.VMEM((n,WIDE,WIDE),f32),
            pltpu.VMEM((1024,1024),f32),pltpu.VMEM((PAD,BLK),f32),pltpu.VMEM((PAD,PAD),bf),
            dma((2,snapshots.shape[1]//CHUNK)),dma((TILES,)),dma,dma,dma((TILES,)),dma((3,)),dma((3,)),dma,dma,dma((n,)),dma((n,)),
        ],
        compiler_params=pltpu.CompilerParams(collective_id=0,has_side_effects=True,vmem_limit_bytes=56*2**20),
        name="fit",
    )(snapshots,basis,jnp.asarray(row_of_column()))
    def finish(a_ref,b_ref,op_ref,res_ref):
        op_ref[...]=a_ref[...]
        res_ref[...]=b_ref[...]
    return pl.pallas_call(
        finish,
        out_shape=(jax.ShapeDtypeStruct((MODES,COLS),f32),jax.ShapeDtypeStruct((MODES,WIDE),f32)),
        in_specs=[pl.BlockSpec(memory_space=pltpu.VMEM)]*2,
        out_specs=(pl.BlockSpec(memory_space=pltpu.VMEM),)*2,
        compiler_params=pltpu.CompilerParams(vmem_limit_bytes=2**20),
        name="finish",
    )(*outs)

def solution(mesh):
    return jax.shard_map(on_device,mesh=mesh,in_specs=(P("tm",("rowa","rowb")),P(None,("rowa","rowb"))),out_specs=(P(),P(None,"tm")),check_vma=False)
```

```python
import functools

import numpy as np
import jax, jax.numpy as jnp
from jax import lax
from jax.experimental import pallas as pl
from jax.experimental.pallas import tpu as pltpu
from jax.sharding import PartitionSpec as P

MODES=40; COLS=861; PAD=896; BLK=128; NB=7; SNAPS=2048; RHS=896
HALF=MODES//2
NN=(((1,),(0,)),((),())); NT=(((1,),(1,)),((),())); TN=(((0,),(0,)),((),()))

def row_of_column():
    rows=np.full((1,PAD),-1,np.int32)
    rows[0,:MODES]=HALF*MODES+np.arange(MODES)
    at=MODES
    for i in range(MODES):
        for j in range(i,MODES):
            d=j-i
            if d<HALF: r=d*MODES+i
            elif d==HALF: r=(HALF+1)*MODES+i
            else: r=(MODES-d)*MODES+j
            rows[0,at]=r; at+=1
    rows[0,at]=COLS-1
    return rows

def split(x):
    hi=x.astype(jnp.bfloat16)
    return hi,(x-hi.astype(jnp.float32)).astype(jnp.bfloat16)

def dot(a,b,dims):
    return lax.dot_general(a,b,dims,preferred_element_type=jnp.float32)

def dot3(a,b,dims):
    ah,al=a; bh,bl=b
    return dot(ah,bh,dims)+(dot(ah,bl,dims)+dot(al,bh,dims))

def spread_row(x,k): return jnp.broadcast_to(x[k:k+1,:],(8,BLK))
def spread_col(x,c): return jnp.broadcast_to(x[:,c:c+1],(8,BLK))

def row_of(x,k): return spread_row(x[k//8],k%8)

def eliminate(cols,rows):
    n=len(cols)
    sub=lax.broadcasted_iota(jnp.int32,(8,BLK),0)
    scale=[jnp.zeros((8,BLK),jnp.float32) for _ in rows]
    def step(k,r,rows):
        on=sub==k%8
        m=list(cols[k])
        m[k//8]=jnp.where(on,0.0,m[k//8])
        m=[x*r for x in m]
        scale[k//8]=jnp.where(on,r,scale[k//8])
        def less(x):
            t=row_of(x,k)
            return [x[q]-m[q]*t for q in range(len(x))]
        for j in range(k+1,n): cols[j]=less(cols[j])
        return less(rows)
    for k in range(0,n,2):
        p=row_of(cols[k],k)
        det=p*row_of(cols[k+1],k+1)-row_of(cols[k],k+1)*row_of(cols[k+1],k)
        r,r2=1.0/p,p*(1.0/det)
        rows=step(k,r,rows)
        rows=step(k+1,r2,rows)
    return [rows[q]*scale[q] for q in range(len(rows))]

def inverse(a,between):
    a=list(a)
    bf=jnp.bfloat16
    sub=lax.broadcasted_iota(jnp.int32,(8,BLK),0)
    lane=lax.broadcasted_iota(jnp.int32,(8,BLK),1)
    for s in range(8):
        at,nxt=(2*s,2*s+1),((2*s+2,2*s+3) if s<7 else ())
        inblk=(lane>=16*s)&(lane<16*s+16)
        cols=[[spread_col(a[i],16*s+k) for i in at] for k in range(16)]
        rows=[jnp.where(inblk,jnp.where(lane-16*s==sub+8*q,1.0,0.0),a[i]) for q,i in enumerate(at)]
        rows=eliminate(cols,rows)
        def pad(v):
            return jnp.concatenate(([jnp.zeros((16*s,BLK),bf)] if s else [])+[v]+([jnp.zeros((112-16*s,BLK),bf)] if s<7 else []),axis=0)
        far=[i for i in range(16) if i not in at+nxt]
        upd=dot3(split(jnp.concatenate([a[i] for i in far],axis=0)),tuple(pad(v) for v in split(jnp.concatenate(rows,axis=0))),NN)
        new=list(a)
        for n,i in enumerate(far):
            new[i]=jnp.where(inblk,0.0,a[i])-upd[8*n:8*n+8]
        if nxt:
            V=[row_of(rows,k) for k in range(16)]
        for i in nxt:
            p=[spread_col(a[i],16*s+k)*V[k] for k in range(16)]
            while len(p)>1: p=[p[2*q]+p[2*q+1] for q in range(len(p)//2)]
            new[i]=jnp.where(inblk,0.0,a[i])-p[0]
        for q,i in enumerate(at): new[i]=rows[q]
        a=new
        between(s)
    return jnp.concatenate(a,axis=0)


MESH=pl.DeviceIdType.MESH
TILES=10
PLANE=32
ORDER=(0,1,2,3,7,6,5,4)
AT=(5,6,7)
CHUNK=1024
WIDE=256
LATER={(1,0):(1,1),(1,2):(1,2),(1,4):(1,3),(2,0):(2,2),(2,3):(2,3),(3,1):(3,3)}

def put(hi,lo,at,cols,x):
    h,l=split(x)
    hi[at:at+x.shape[0],cols]=h
    lo[at:at+x.shape[0],cols]=l

def kept(first):
    return first+lax.broadcasted_iota(jnp.int32,(1,WIDE),1)<SNAPS-1

def features(hi,lo,twice,slot,block):
    keep=kept(WIDE*slot)
    now=jnp.where(keep,block,0.0)
    twice[0:MODES,:]=now
    twice[MODES:2*MODES,:]=now
    cols=pl.ds(pl.multiple_of(WIDE*slot,WIDE),WIDE)
    for d in range(0,HALF,2):
        put(hi,lo,d*MODES,cols,jnp.concatenate([now*twice[d:d+MODES,:],now*twice[d+1:d+1+MODES,:]],axis=0))
    sub=lax.broadcasted_iota(jnp.int32,(24,WIDE),0)
    last=jnp.where(sub<HALF,twice[0:24,:]*twice[HALF:HALF+24,:],jnp.where((sub==HALF)&keep,1.0,0.0))
    put(hi,lo,800,cols,jnp.concatenate([now,last,jnp.zeros((32,WIDE),jnp.float32)],axis=0))

def targets(hi,lo,slot,block,edge):
    lane=lax.broadcasted_iota(jnp.int32,(MODES,WIDE),1)
    ahead=jnp.concatenate([block[:,1:],block[:,:1]],axis=1)
    ahead=jnp.where(lane==WIDE-1,jnp.broadcast_to(edge[:,0:1],(MODES,WIDE)),ahead)
    ahead=jnp.where(kept(WIDE*slot),ahead,0.0)
    cols=pl.ds(pl.multiple_of(WIDE*slot,WIDE),WIDE)
    put(hi,lo,RHS,cols,jnp.concatenate([ahead,jnp.zeros((88,WIDE),jnp.float32)],axis=0))

def product(hi,lo,piece):
    r,c=(slice(WIDE*x,WIDE*x+WIDE) for x in piece)
    return dot3((hi[r,:],lo[r,:]),(hi[c,:],lo[c,:]),NT)

def solve(sys,sol,between):
    sub=lax.broadcasted_iota(jnp.int32,(BLK,BLK),0)
    diag=sub==lax.broadcasted_iota(jnp.int32,(BLK,BLK),1)
    for k in range(NB):
        at=slice(BLK*k,BLK*k+BLK)
        row=sub+BLK*k
        pen=jnp.where((row<800)|((row>=840)&(row<860)),0.1*SNAPS,jnp.where(row<COLS,0.01*SNAPS,1.0)).astype(jnp.float32)
        D=sys[at,at]+jnp.where(diag,pen,0.0)
        inv=inverse([D[8*i:8*i+8,:] for i in range(16)],functools.partial(between,k))
        rest=slice(BLK*k+BLK,PAD+BLK)
        Rs=split(sys[at,rest])
        W=dot3(split(inv),Rs,NN)
        Ws=split(W)
        sys[at,rest]=W
        for i in range(k+1,NB):
            o=BLK*(i-k-1)
            upd=dot3((Rs[0][:,o:o+BLK],Rs[1][:,o:o+BLK]),(Ws[0][:,o:],Ws[1][:,o:]),TN)
            if k==0 and i>1:
                sys[BLK*i:BLK*i+BLK,BLK*i:]=-upd
            else:
                sys[BLK*i:BLK*i+BLK,BLK*i:]=sys[BLK*i:BLK*i+BLK,BLK*i:]-upd
    for k in range(NB-1,-1,-1):
        at=slice(BLK*k,BLK*k+BLK)
        x=sys[at,RHS:]
        if k<NB-1:
            x=x-dot3(split(sys[at,BLK*k+BLK:RHS]),split(sol[BLK*k+BLK:,:]),NN)
        sol[at,:]=x

def kernel(snap_ref,basis_ref,rowof_ref,op_ref,res_ref,
           snap,basis,part,terms,blocks,others,twice,hi,lo,sys,sol,perm,
           load_sem,scatter_send,scatter_recv,spread_send,spread_recv,time_send,time_recv,edge_send,edge_recv):
    tm=lax.axis_index("tm")
    rowa=lax.axis_index("rowa")
    rowb=lax.axis_index("rowb")
    here=rowa*4+rowb
    x,core=tm//2,lax.rem(tm,2)
    chunks=snap.shape[1]//CHUNK
    loads=[]
    for c in range(chunks):
        at=pl.ds(c*CHUNK,CHUNK)
        pair=(pltpu.make_async_copy(snap_ref.at[:,at],snap.at[:,at],load_sem.at[0,c]),
              pltpu.make_async_copy(basis_ref.at[:,at],basis.at[:,at],load_sem.at[1,c]))
        for y in pair: y.start()
        loads.append(pair)
    def plane_id(q): return {"rowa":q//4,"rowb":lax.rem(q,4)}
    def time_id(i): return {"tm":lax.rem(tm+i,8)}
    def owner(t):
        return 4*(AT[t//4]+core*(11-2*AT[t//4]))+t%4
    turn=lax.rem(rowa+core*(11-2*rowa)+3,8)
    tile=4*turn+rowb
    owns=tile<TILES
    barrier=pltpu.get_barrier_semaphore()
    def greet(device):
        pl.semaphore_signal(barrier,inc=1,device_id=device,device_id_type=MESH)
    @pl.when(owns)
    def _():
        for a in (4,5,6,7,3,2,1,0):
            for b in range(4):
                @pl.when(4*a+b!=here)
                def _(): greet({"rowa":a,"rowb":b})
    @pl.when(jnp.logical_not(owns))
    def _():
        for t in range(TILES): greet(plane_id(owner(t)))
    for i in range(1,8): greet(time_id(i))
    total=jnp.zeros((MODES,WIDE),jnp.float32)
    for c in range(chunks):
        for y in loads[c]: y.wait()
        at=slice(c*CHUNK,c*CHUNK+CHUNK)
        total=total+dot(basis[:,at],snap[:,at],NT)
    for t in range(TILES):
        g,h=t//2,t%2
        part[t]=total[8*g:8*g+8,128*h:128*h+128]
    @pl.when(owns)
    def _(): pl.semaphore_wait(barrier,PLANE-1+7)
    @pl.when(jnp.logical_not(owns))
    def _(): pl.semaphore_wait(barrier,TILES+7)

    def scatter(t):
        return pltpu.make_async_remote_copy(src_ref=part.at[t],dst_ref=terms.at[here],send_sem=scatter_send.at[t],recv_sem=scatter_recv,device_id=plane_id(owner(t)),device_id_type=MESH)
    def spread(a,b):
        ref=blocks.at[x,pl.ds(pl.multiple_of(8*(tile//2),8),8),pl.ds(pl.multiple_of(128*lax.rem(tile,2),128),128)]
        return pltpu.make_async_remote_copy(src_ref=ref,dst_ref=ref,send_sem=spread_send,recv_sem=spread_recv.at[tile],device_id={"rowa":a,"rowb":b},device_id_type=MESH)
    for t in range(TILES):
        @pl.when(owner(t)!=here)
        def _(): scatter(t).start()
    @pl.when(owns)
    def _():
        pltpu.make_async_copy(terms.at[0:PLANE-1],terms.at[0:PLANE-1],scatter_recv).wait()
        terms[here]=part[tile]
        sums=[terms[q] for q in range(PLANE)]
        while len(sums)>1: sums=[sums[2*q]+sums[2*q+1] for q in range(len(sums)//2)]
        blocks[x,pl.ds(pl.multiple_of(8*(tile//2),8),8),pl.ds(pl.multiple_of(128*lax.rem(tile,2),128),128)]=sums[0]
        for a in ORDER:
            for b in range(4):
                @pl.when(4*a+b!=here)
                def _(): spread(a,b).start()
    perm[...]=jnp.where(lax.broadcasted_iota(jnp.int32,(PAD,PAD),0)==rowof_ref[...],1.0,0.0).astype(jnp.bfloat16)
    for t in range(TILES):
        @pl.when(owner(t)!=here)
        def _():
            ref=blocks.at[x,8*(t//2):8*(t//2)+8,128*(t%2):128*(t%2)+128]
            pltpu.make_async_remote_copy(src_ref=ref,dst_ref=ref,send_sem=spread_send,recv_sem=spread_recv.at[t],device_id=plane_id(owner(t)),device_id_type=MESH).wait_recv()

    def to_same(d):
        ref=blocks.at[x]
        return pltpu.make_async_remote_copy(src_ref=ref,dst_ref=ref,send_sem=time_send.at[d-1],recv_sem=time_recv.at[d-1],device_id={"tm":2*lax.rem(x+d,4)+core},device_id_type=MESH)
    for d in (2,1,3): to_same(d).start()
    def to_other():
        return pltpu.make_async_remote_copy(src_ref=blocks,dst_ref=others,send_sem=edge_send,recv_sem=edge_recv,device_id={"tm":tm+1-2*core},device_id_type=MESH)
    def arrival(d):
        ref=blocks.at[lax.rem(x+4-d,4)]
        return pltpu.make_async_remote_copy(src_ref=ref,dst_ref=ref,send_sem=time_send.at[d-1],recv_sem=time_recv.at[d-1],device_id={"tm":2*lax.rem(x+d,4)+core},device_id_type=MESH)
    def own(of): features(hi,lo,twice,2*of+core,blocks[of])
    own(x)
    for d in (1,2,3): arrival(d).wait_recv()
    to_other().start()
    for of in range(4):
        @pl.when(of!=x)
        def _(): own(of)
    to_other().wait_recv()
    for of in range(4):
        features(hi,lo,twice,2*of+1-core,others[of])
        targets(hi,lo,2*of+core,blocks[of],others[lax.rem(of+core,4),:,0:128])
        targets(hi,lo,2*of+1-core,others[of],blocks[lax.rem(of+1-core,4),:,0:128])
    def fill(i,j):
        p=product(hi,lo,(i,j))
        r,c=WIDE*i,WIDE*j
        if i==0:
            sys[r:r+WIDE,c:c+WIDE]=p
        elif i<j:
            sys[r:r+WIDE,c:c+WIDE]=sys[r:r+WIDE,c:c+WIDE]+p
        else:
            sys[r:r+BLK,c:c+WIDE]=sys[r:r+BLK,c:c+WIDE]+p[0:BLK]
            sys[r+BLK:r+WIDE,c+BLK:c+WIDE]=sys[r+BLK:r+WIDE,c+BLK:c+WIDE]+p[BLK:WIDE,BLK:WIDE]
    fill(0,0)
    fill(0,1)
    fill(0,2)
    fill(0,3)
    def between(k,s):
        if (k,s) in LATER: fill(*LATER[k,s])
    solve(sys,sol,between)

    X=sol[...]
    Xs=split(X)
    cols=pl.ds(pl.multiple_of(WIDE*tm,WIDE),WIDE)
    fit=dot3(Xs,(hi[0:PAD,cols],lo[0:PAD,cols]),TN)
    ahead=hi[RHS:RHS+48,cols].astype(jnp.float32)+lo[RHS:RHS+48,cols].astype(jnp.float32)
    res_ref[...]=(ahead-fit[0:48,:])[0:MODES,:]
    out=dot(Xs[0],perm[...],TN)+dot(Xs[1],perm[...],TN)
    op_ref[...]=out[0:MODES,0:COLS]
    for t in range(TILES):
        @pl.when(owner(t)!=here)
        def _(): scatter(t).wait_send()
    @pl.when(owns)
    def _(): pltpu.make_async_copy(terms.at[0:PLANE-1],terms.at[0:PLANE-1],spread_send).wait()
    for d in (1,2,3): to_same(d).wait_send()
    to_other().wait_send()

def on_device(snapshots,basis):
    f32,bf=jnp.float32,jnp.bfloat16
    dma=pltpu.SemaphoreType.DMA
    outs=pl.pallas_call(
        kernel,
        out_shape=(jax.ShapeDtypeStruct((MODES,COLS),f32),jax.ShapeDtypeStruct((MODES,WIDE),f32)),
        in_specs=[pl.BlockSpec(memory_space=pltpu.HBM)]*2+[pl.BlockSpec(memory_space=pltpu.VMEM)],
        out_specs=(pl.BlockSpec(memory_space=pltpu.VMEM),)*2,
        scratch_shapes=[
            pltpu.VMEM(snapshots.shape,bf),pltpu.VMEM(basis.shape,bf),
            pltpu.VMEM((TILES,8,128),f32),pltpu.VMEM((PLANE,8,128),f32),
            pltpu.VMEM((4,MODES,WIDE),f32),pltpu.VMEM((4,MODES,WIDE),f32),
            pltpu.VMEM((2*MODES,WIDE),f32),
            pltpu.VMEM((1024,8*WIDE),bf),pltpu.VMEM((1024,8*WIDE),bf),

            pltpu.VMEM((1024,1024),f32),pltpu.VMEM((PAD,BLK),f32),pltpu.VMEM((PAD,PAD),bf),
            dma((2,snapshots.shape[1]//CHUNK)),dma((TILES,)),dma,dma,dma((TILES,)),dma((3,)),dma((3,)),dma,dma,
        ],
        compiler_params=pltpu.CompilerParams(collective_id=0,has_side_effects=True,vmem_limit_bytes=56*2**20),
        name="fit",
    )(snapshots,basis,jnp.asarray(row_of_column()))
    def finish(a_ref,b_ref,op_ref,res_ref,sem):
        copies=(pltpu.make_async_copy(a_ref,op_ref,sem.at[0]),pltpu.make_async_copy(b_ref,res_ref,sem.at[1]))
        for c in copies: c.start()
        for c in copies: c.wait()
    return pl.pallas_call(
        finish,
        out_shape=(jax.ShapeDtypeStruct((MODES,COLS),f32),jax.ShapeDtypeStruct((MODES,WIDE),f32)),
        in_specs=[pl.BlockSpec(memory_space=pltpu.HBM)]*2,
        out_specs=(pl.BlockSpec(memory_space=pltpu.VMEM),)*2,
        scratch_shapes=[dma((2,))],
        name="finish",
    )(*outs)

def solution(mesh):
    return jax.shard_map(on_device,mesh=mesh,in_specs=(P("tm",("rowa","rowb")),P(None,("rowa","rowb"))),out_specs=(P(),P(None,"tm")),check_vma=False)
```

```python
import functools

import numpy as np
import jax, jax.numpy as jnp
from jax import lax
from jax.experimental import pallas as pl
from jax.experimental.pallas import tpu as pltpu
from jax.sharding import PartitionSpec as P

MODES=40; COLS=861; PAD=896; BLK=128; NB=7; SNAPS=2048; RHS=896
HALF=MODES//2
NN=(((1,),(0,)),((),())); NT=(((1,),(1,)),((),())); TN=(((0,),(0,)),((),()))

def row_of_column():
    rows=np.full((1,PAD),-1,np.int32)
    rows[0,:MODES]=HALF*MODES+np.arange(MODES)
    at=MODES
    for i in range(MODES):
        for j in range(i,MODES):
            d=j-i
            if d<HALF: r=d*MODES+i
            elif d==HALF: r=(HALF+1)*MODES+i
            else: r=(MODES-d)*MODES+j
            rows[0,at]=r; at+=1
    rows[0,at]=COLS-1
    return rows

def split(x):
    hi=x.astype(jnp.bfloat16)
    return hi,(x-hi.astype(jnp.float32)).astype(jnp.bfloat16)

def dot(a,b,dims):
    return lax.dot_general(a,b,dims,preferred_element_type=jnp.float32)

def dot3(a,b,dims):
    ah,al=a; bh,bl=b
    return dot(ah,bh,dims)+(dot(ah,bl,dims)+dot(al,bh,dims))

def spread_row(x,k): return jnp.broadcast_to(x[k:k+1,:],(8,BLK))
def spread_col(x,c): return jnp.broadcast_to(x[:,c:c+1],(8,BLK))

def row_of(x,k): return spread_row(x[k//8],k%8)

def eliminate(cols,rows):
    n=len(cols)
    sub=lax.broadcasted_iota(jnp.int32,(8,BLK),0)
    scale=[jnp.zeros((8,BLK),jnp.float32) for _ in rows]
    def step(k,r,rows):
        on=sub==k%8
        m=list(cols[k])
        m[k//8]=jnp.where(on,0.0,m[k//8])
        m=[x*r for x in m]
        scale[k//8]=jnp.where(on,r,scale[k//8])
        def less(x):
            t=row_of(x,k)
            return [x[q]-m[q]*t for q in range(len(x))]
        for j in range(k+1,n): cols[j]=less(cols[j])
        return less(rows)
    for k in range(0,n,2):
        p=row_of(cols[k],k)
        det=p*row_of(cols[k+1],k+1)-row_of(cols[k],k+1)*row_of(cols[k+1],k)
        r,r2=1.0/p,p*(1.0/det)
        rows=step(k,r,rows)
        rows=step(k+1,r2,rows)
    return [rows[q]*scale[q] for q in range(len(rows))]

def inverse(a,between):
    a=list(a)
    bf=jnp.bfloat16
    sub=lax.broadcasted_iota(jnp.int32,(8,BLK),0)
    lane=lax.broadcasted_iota(jnp.int32,(8,BLK),1)
    for s in range(8):
        at,nxt=(2*s,2*s+1),((2*s+2,2*s+3) if s<7 else ())
        inblk=(lane>=16*s)&(lane<16*s+16)
        cols=[[spread_col(a[i],16*s+k) for i in at] for k in range(16)]
        rows=[jnp.where(inblk,jnp.where(lane-16*s==sub+8*q,1.0,0.0),a[i]) for q,i in enumerate(at)]
        rows=eliminate(cols,rows)
        def pad(v):
            return jnp.concatenate(([jnp.zeros((16*s,BLK),bf)] if s else [])+[v]+([jnp.zeros((112-16*s,BLK),bf)] if s<7 else []),axis=0)
        far=[i for i in range(16) if i not in at+nxt]
        upd=dot3(split(jnp.concatenate([a[i] for i in far],axis=0)),tuple(pad(v) for v in split(jnp.concatenate(rows,axis=0))),NN)
        new=list(a)
        for n,i in enumerate(far):
            new[i]=jnp.where(inblk,0.0,a[i])-upd[8*n:8*n+8]
        if nxt:
            V=[row_of(rows,k) for k in range(16)]
        for i in nxt:
            p=[spread_col(a[i],16*s+k)*V[k] for k in range(16)]
            while len(p)>1: p=[p[2*q]+p[2*q+1] for q in range(len(p)//2)]
            new[i]=jnp.where(inblk,0.0,a[i])-p[0]
        for q,i in enumerate(at): new[i]=rows[q]
        a=new
        between(s)
    return jnp.concatenate(a,axis=0)


MESH=pl.DeviceIdType.MESH
TILES=10
PLANE=32
ORDER=(0,1,2,3,7,6,5,4)
AT=(6,7,8)
CHUNK=1024
WIDE=256
LATER={(1,0):(1,1),(1,2):(1,2),(1,4):(1,3),(2,0):(2,2),(2,3):(2,3),(3,1):(3,3)}

def put(hi,lo,at,cols,x):
    h,l=split(x)
    hi[at:at+x.shape[0],cols]=h
    lo[at:at+x.shape[0],cols]=l

def kept(first):
    return first+lax.broadcasted_iota(jnp.int32,(1,WIDE),1)<SNAPS-1

def features(hi,lo,twice,slot,block):
    keep=kept(WIDE*slot)
    now=jnp.where(keep,block,0.0)
    twice[0:MODES,:]=now
    twice[MODES:2*MODES,:]=now
    cols=pl.ds(pl.multiple_of(WIDE*slot,WIDE),WIDE)
    for d in range(0,HALF,2):
        put(hi,lo,d*MODES,cols,jnp.concatenate([now*twice[d:d+MODES,:],now*twice[d+1:d+1+MODES,:]],axis=0))
    sub=lax.broadcasted_iota(jnp.int32,(24,WIDE),0)
    last=jnp.where(sub<HALF,twice[0:24,:]*twice[HALF:HALF+24,:],jnp.where((sub==HALF)&keep,1.0,0.0))
    put(hi,lo,800,cols,jnp.concatenate([now,last,jnp.zeros((32,WIDE),jnp.float32)],axis=0))

def targets(hi,lo,slot,block,edge):
    lane=lax.broadcasted_iota(jnp.int32,(MODES,WIDE),1)
    ahead=jnp.concatenate([block[:,1:],block[:,:1]],axis=1)
    ahead=jnp.where(lane==WIDE-1,jnp.broadcast_to(edge[:,0:1],(MODES,WIDE)),ahead)
    ahead=jnp.where(kept(WIDE*slot),ahead,0.0)
    cols=pl.ds(pl.multiple_of(WIDE*slot,WIDE),WIDE)
    put(hi,lo,RHS,cols,jnp.concatenate([ahead,jnp.zeros((88,WIDE),jnp.float32)],axis=0))

def product(hi,lo,piece):
    r,c=(slice(WIDE*x,WIDE*x+WIDE) for x in piece)
    return dot3((hi[r,:],lo[r,:]),(hi[c,:],lo[c,:]),NT)

def solve(sys,sol,between):
    sub=lax.broadcasted_iota(jnp.int32,(BLK,BLK),0)
    diag=sub==lax.broadcasted_iota(jnp.int32,(BLK,BLK),1)
    for k in range(NB):
        at=slice(BLK*k,BLK*k+BLK)
        row=sub+BLK*k
        pen=jnp.where((row<800)|((row>=840)&(row<860)),0.1*SNAPS,jnp.where(row<COLS,0.01*SNAPS,1.0)).astype(jnp.float32)
        D=sys[at,at]+jnp.where(diag,pen,0.0)
        inv=inverse([D[8*i:8*i+8,:] for i in range(16)],functools.partial(between,k))
        rest=slice(BLK*k+BLK,PAD+BLK)
        Rs=split(sys[at,rest])
        W=dot3(split(inv),Rs,NN)
        Ws=split(W)
        sys[at,rest]=W
        for i in range(k+1,NB):
            o=BLK*(i-k-1)
            upd=dot3((Rs[0][:,o:o+BLK],Rs[1][:,o:o+BLK]),(Ws[0][:,o:],Ws[1][:,o:]),TN)
            if k==0 and i>1:
                sys[BLK*i:BLK*i+BLK,BLK*i:]=-upd
            else:
                sys[BLK*i:BLK*i+BLK,BLK*i:]=sys[BLK*i:BLK*i+BLK,BLK*i:]-upd
    for k in range(NB-1,-1,-1):
        at=slice(BLK*k,BLK*k+BLK)
        x=sys[at,RHS:]
        if k<NB-1:
            x=x-dot3(split(sys[at,BLK*k+BLK:RHS]),split(sol[BLK*k+BLK:,:]),NN)
        sol[at,:]=x

def kernel(snap_ref,basis_ref,rowof_ref,op_ref,res_ref,
           snap,basis,part,terms,blocks,others,twice,hi,lo,sys,sol,perm,
           load_sem,scatter_send,scatter_recv,spread_send,spread_recv,time_send,time_recv,edge_send,edge_recv):
    tm=lax.axis_index("tm")
    rowa=lax.axis_index("rowa")
    rowb=lax.axis_index("rowb")
    here=rowa*4+rowb
    x,core=tm//2,lax.rem(tm,2)
    chunks=snap.shape[1]//CHUNK
    loads=[]
    for c in range(chunks):
        at=pl.ds(c*CHUNK,CHUNK)
        pair=(pltpu.make_async_copy(snap_ref.at[:,at],snap.at[:,at],load_sem.at[0,c]),
              pltpu.make_async_copy(basis_ref.at[:,at],basis.at[:,at],load_sem.at[1,c]))
        for y in pair: y.start()
        loads.append(pair)
    def plane_id(q): return {"rowa":q//4,"rowb":lax.rem(q,4)}
    def time_id(i): return {"tm":lax.rem(tm+i,8)}
    def owner(t):
        return 4*lax.rem(AT[t//4]+core*(21-2*AT[t//4]),8)+t%4
    turn=lax.rem(rowa+core*(21-2*rowa)+2,8)
    tile=4*turn+rowb
    owns=tile<TILES
    barrier=pltpu.get_barrier_semaphore()
    def greet(device):
        pl.semaphore_signal(barrier,inc=1,device_id=device,device_id_type=MESH)
    @pl.when(owns)
    def _():
        for a in (4,5,6,7,3,2,1,0):
            for b in range(4):
                @pl.when(4*a+b!=here)
                def _(): greet({"rowa":a,"rowb":b})
    @pl.when(jnp.logical_not(owns))
    def _():
        for t in range(TILES): greet(plane_id(owner(t)))
    for i in range(1,8): greet(time_id(i))
    total=jnp.zeros((MODES,WIDE),jnp.float32)
    for c in range(chunks):
        for y in loads[c]: y.wait()
        at=slice(c*CHUNK,c*CHUNK+CHUNK)
        total=total+dot(basis[:,at],snap[:,at],NT)
    for t in range(TILES):
        g,h=t//2,t%2
        part[t]=total[8*g:8*g+8,128*h:128*h+128]
    @pl.when(owns)
    def _(): pl.semaphore_wait(barrier,PLANE-1+7)
    @pl.when(jnp.logical_not(owns))
    def _(): pl.semaphore_wait(barrier,TILES+7)

    def scatter(t):
        return pltpu.make_async_remote_copy(src_ref=part.at[t],dst_ref=terms.at[here],send_sem=scatter_send.at[t],recv_sem=scatter_recv,device_id=plane_id(owner(t)),device_id_type=MESH)
    def spread(a,b):
        ref=blocks.at[x,pl.ds(pl.multiple_of(8*(tile//2),8),8),pl.ds(pl.multiple_of(128*lax.rem(tile,2),128),128)]
        return pltpu.make_async_remote_copy(src_ref=ref,dst_ref=ref,send_sem=spread_send,recv_sem=spread_recv.at[tile],device_id={"rowa":a,"rowb":b},device_id_type=MESH)
    for t in range(TILES):
        @pl.when(owner(t)!=here)
        def _(): scatter(t).start()
    @pl.when(owns)
    def _():
        pltpu.make_async_copy(terms.at[0:PLANE-1],terms.at[0:PLANE-1],scatter_recv).wait()
        terms[here]=part[tile]
        sums=[terms[q] for q in range(PLANE)]
        while len(sums)>1: sums=[sums[2*q]+sums[2*q+1] for q in range(len(sums)//2)]
        blocks[x,pl.ds(pl.multiple_of(8*(tile//2),8),8),pl.ds(pl.multiple_of(128*lax.rem(tile,2),128),128)]=sums[0]
        for a in ORDER:
            for b in range(4):
                @pl.when(4*a+b!=here)
                def _(): spread(a,b).start()
    perm[...]=jnp.where(lax.broadcasted_iota(jnp.int32,(PAD,PAD),0)==rowof_ref[...],1.0,0.0).astype(jnp.bfloat16)
    for t in range(TILES):
        @pl.when(owner(t)!=here)
        def _():
            ref=blocks.at[x,8*(t//2):8*(t//2)+8,128*(t%2):128*(t%2)+128]
            pltpu.make_async_remote_copy(src_ref=ref,dst_ref=ref,send_sem=spread_send,recv_sem=spread_recv.at[t],device_id=plane_id(owner(t)),device_id_type=MESH).wait_recv()

    def to_same(d):
        ref=blocks.at[x]
        return pltpu.make_async_remote_copy(src_ref=ref,dst_ref=ref,send_sem=time_send.at[d-1],recv_sem=time_recv.at[d-1],device_id={"tm":2*lax.rem(x+d,4)+core},device_id_type=MESH)
    for d in (2,1,3): to_same(d).start()
    def to_other():
        return pltpu.make_async_remote_copy(src_ref=blocks,dst_ref=others,send_sem=edge_send,recv_sem=edge_recv,device_id={"tm":tm+1-2*core},device_id_type=MESH)
    def arrival(d):
        ref=blocks.at[lax.rem(x+4-d,4)]
        return pltpu.make_async_remote_copy(src_ref=ref,dst_ref=ref,send_sem=time_send.at[d-1],recv_sem=time_recv.at[d-1],device_id={"tm":2*lax.rem(x+d,4)+core},device_id_type=MESH)
    def own(of): features(hi,lo,twice,2*of+core,blocks[of])
    own(x)
    for d in (1,2,3): arrival(d).wait_recv()
    to_other().start()
    for of in range(4):
        @pl.when(of!=x)
        def _(): own(of)
    to_other().wait_recv()
    for of in range(4):
        features(hi,lo,twice,2*of+1-core,others[of])
        targets(hi,lo,2*of+core,blocks[of],others[lax.rem(of+core,4),:,0:128])
        targets(hi,lo,2*of+1-core,others[of],blocks[lax.rem(of+1-core,4),:,0:128])
    def fill(i,j):
        p=product(hi,lo,(i,j))
        r,c=WIDE*i,WIDE*j
        if i==0:
            sys[r:r+WIDE,c:c+WIDE]=p
        elif i<j:
            sys[r:r+WIDE,c:c+WIDE]=sys[r:r+WIDE,c:c+WIDE]+p
        else:
            sys[r:r+BLK,c:c+WIDE]=sys[r:r+BLK,c:c+WIDE]+p[0:BLK]
            sys[r+BLK:r+WIDE,c+BLK:c+WIDE]=sys[r+BLK:r+WIDE,c+BLK:c+WIDE]+p[BLK:WIDE,BLK:WIDE]
    fill(0,0)
    fill(0,1)
    fill(0,2)
    fill(0,3)
    def between(k,s):
        if (k,s) in LATER: fill(*LATER[k,s])
    solve(sys,sol,between)

    X=sol[:,0:48]
    Xs=split(X)
    cols=pl.ds(pl.multiple_of(WIDE*tm,WIDE),WIDE)
    fit=dot3(Xs,(hi[0:PAD,cols],lo[0:PAD,cols]),TN)
    ahead=hi[RHS:RHS+48,cols].astype(jnp.float32)+lo[RHS:RHS+48,cols].astype(jnp.float32)
    res_ref[...]=(ahead-fit)[0:MODES,:]
    out=dot(Xs[0],perm[...],TN)+dot(Xs[1],perm[...],TN)
    op_ref[...]=out[0:MODES,0:COLS]
    for t in range(TILES):
        @pl.when(owner(t)!=here)
        def _(): scatter(t).wait_send()
    @pl.when(owns)
    def _(): pltpu.make_async_copy(terms.at[0:PLANE-1],terms.at[0:PLANE-1],spread_send).wait()
    for d in (1,2,3): to_same(d).wait_send()
    to_other().wait_send()

def on_device(snapshots,basis):
    f32,bf=jnp.float32,jnp.bfloat16
    dma=pltpu.SemaphoreType.DMA
    outs=pl.pallas_call(
        kernel,
        out_shape=(jax.ShapeDtypeStruct((MODES,COLS),f32),jax.ShapeDtypeStruct((MODES,WIDE),f32)),
        in_specs=[pl.BlockSpec(memory_space=pltpu.HBM)]*2+[pl.BlockSpec(memory_space=pltpu.VMEM)],
        out_specs=(pl.BlockSpec(memory_space=pltpu.VMEM),)*2,
        scratch_shapes=[
            pltpu.VMEM(snapshots.shape,bf),pltpu.VMEM(basis.shape,bf),
            pltpu.VMEM((TILES,8,128),f32),pltpu.VMEM((PLANE,8,128),f32),
            pltpu.VMEM((4,MODES,WIDE),f32),pltpu.VMEM((4,MODES,WIDE),f32),
            pltpu.VMEM((2*MODES,WIDE),f32),
            pltpu.VMEM((1024,8*WIDE),bf),pltpu.VMEM((1024,8*WIDE),bf),

            pltpu.VMEM((1024,1024),f32),pltpu.VMEM((PAD,BLK),f32),pltpu.VMEM((PAD,PAD),bf),
            dma((2,snapshots.shape[1]//CHUNK)),dma((TILES,)),dma,dma,dma((TILES,)),dma((3,)),dma((3,)),dma,dma,
        ],
        compiler_params=pltpu.CompilerParams(collective_id=0,has_side_effects=True,vmem_limit_bytes=56*2**20),
        name="fit",
    )(snapshots,basis,jnp.asarray(row_of_column()))
    def finish(a_ref,b_ref,op_ref,res_ref,sem):
        copies=(pltpu.make_async_copy(a_ref,op_ref,sem.at[0]),pltpu.make_async_copy(b_ref,res_ref,sem.at[1]))
        for c in copies: c.start()
        for c in copies: c.wait()
    return pl.pallas_call(
        finish,
        out_shape=(jax.ShapeDtypeStruct((MODES,COLS),f32),jax.ShapeDtypeStruct((MODES,WIDE),f32)),
        in_specs=[pl.BlockSpec(memory_space=pltpu.HBM)]*2,
        out_specs=(pl.BlockSpec(memory_space=pltpu.VMEM),)*2,
        scratch_shapes=[dma((2,))],
        name="finish",
    )(*outs)

def solution(mesh):
    return jax.shard_map(on_device,mesh=mesh,in_specs=(P("tm",("rowa","rowb")),P(None,("rowa","rowb"))),out_specs=(P(),P(None,"tm")),check_vma=False)
```
